32 devices in a mesh: uv: 4 (over y, core), channel: 4 (over z), parity: 2 (over x).
Axes of the slice: x: 2, y: 2, z: 4, core: 2. Of those that a mesh axis runs over, the one named last changes fastest.
Arguments:
- visibility: bfloat16 [2, 4, 128, 32, 128], P('parity', 'channel', 'uv'), may hold values from -6 to 6
- kernel: bfloat16 [2, 4, 128, 128, 256], P('parity', 'channel', 'uv'), may hold values from -0.5 to 0.5
- block_tile: int32 [2, 4, 128], P('parity', 'channel', 'uv'), may hold values from 0 to 255, as said below
- block_chan: int32 [2, 4, 128], P('parity', 'channel', 'uv'), may hold values from 0 to 240
- tile_owner: int32 [256], replicated, may hold values from 0 to 3, as said below
- inv_cov: bfloat16 [1024, 1024], replicated, as said below
Outputs:
- cross_power: float32 [1024, 65536], P(None, ('uv', 'channel', 'parity'))
- diff_power: float32 [1024, 65536], P(None, ('uv', 'channel', 'parity'))
The draws below stay inside these ranges and needn't reach their ends.
Inputs may be any that keep to these rules, and one draw needn't show every extreme that they name: `tile_owner`: each owner index owns exactly 64 tiles. `block_tile`: call slot(t) // 16 the cell group of tile t. Among the 32 blocks of one device (one aligned run along the last dimension), at most 4 name tiles of the same owner and the same cell group. `inv_cov`: entries are finite.
All inputs are finite; a program needn't handle non-finite values.
Results may differ from the reference program's by a relative error of at most 0.0067.
Values may be sent and summed in bfloat16 or wider, within the bound.
A program may use at most 192 MiB of HBM per device.

```python
import math
import jax
import jax.numpy as jnp
from jax import lax

NCH = 1024
PIX = 256
CHB = 16
BV = 128
NB = 32
TILE_DEV = 64
CH_DEV = 256
TILES = 256
TPC = 16
CELLS = 65536
DESTS = 16
SLOTS = 4
BLOCKS = 128
N_UV = 4
N_CHANNEL = 4


def owner_table(key):
    ranking = jax.random.permutation(jax.random.fold_in(key, 7), TILES)
    return (ranking // TILE_DEV).astype(jnp.int32)


def draw_tile_owner(key, part):
    return owner_table(key)


def draw_block_tile(key, part):
    owners_all = owner_table(key)
    indices = jnp.arange(TILES, dtype=jnp.int32)
    listing = jnp.argsort(owners_all * TILES + indices).astype(jnp.int32)
    hot_dest = jax.random.randint(jax.random.fold_in(key, 13), (), 0, DESTS).astype(jnp.int32)
    dev_keys = jax.random.split(jax.random.fold_in(key, 17), 2 * N_CHANNEL * N_UV)

    def device_blocks(subkey):
        key_perm, key_order, key_pick = jax.random.split(subkey, 3)
        spares = jax.random.permutation(key_perm, (DESTS - 1) * SLOTS)[:NB - SLOTS] // SLOTS
        spares = spares.astype(jnp.int32)
        spares = spares + (spares >= hot_dest).astype(jnp.int32)
        target = jnp.concatenate([jnp.full((SLOTS,), hot_dest, jnp.int32), spares])
        target = jax.random.permutation(key_order, target)
        choose = jax.random.randint(key_pick, (NB,), 0, TPC).astype(jnp.int32)
        owner_pick = target // N_CHANNEL
        slot_pick = target % N_CHANNEL * TPC + choose
        return listing[owner_pick * TILE_DEV + slot_pick]
    tile_ids = jax.vmap(device_blocks)(dev_keys)
    return tile_ids.reshape(2, N_CHANNEL, N_UV * NB).astype(jnp.int32)


def draw_inv_cov(key, part):
    key_off, key_diag = jax.random.split(jax.random.fold_in(key, 31), 2)
    spread = 0.7 / math.sqrt(NCH)
    offdiag = jax.random.normal(key_off, (NCH, NCH), jnp.float32) * spread
    diagonal = jnp.exp(jax.random.uniform(key_diag, (NCH,), jnp.float32, math.log(0.5), math.log(2.0)))
    matrix = offdiag + jnp.eye(NCH, dtype=jnp.float32) * diagonal[None, :]
    return matrix.astype(jnp.bfloat16)


def set_ends(drawn, own_key, least, high):
    longest = drawn.shape.index(max(drawn.shape))
    spots = []
    for shift in (0, 1):
        where = [jax.random.randint(jax.random.fold_in(own_key, axis), (), 0, length) for axis, length in enumerate(drawn.shape)]
        where[longest] = (where[longest] + shift) % drawn.shape[longest]
        spots.append(tuple(where))
    return drawn.at[spots[0]].set(least).at[spots[1]].set(high)


def levels(stream_key, extent, shards, low, largest):
    gain = 1.0
    for dim, blocks in shards:
        draws = jax.random.uniform(jax.random.fold_in(jax.random.fold_in(stream_key, 6), dim), (blocks,), jnp.float32, low / len(shards), largest / len(shards))
        gain = gain * jnp.repeat(jnp.exp(draws), extent[dim] // blocks).reshape((-1,) + (1,) * (len(extent) - 1 - dim))
    return gain


def centred(rng, extent, scale, reach, shards=(), kind=jnp.bfloat16):
    loudness = levels(rng, extent, shards, -0.22, 0.18) if shards else 1.0
    result = jax.random.normal(rng, extent, jnp.float32) * scale * loudness
    return jnp.minimum(jnp.maximum(result, -reach), reach).astype(kind)


def setup_inputs(seed: int = 0) -> dict:
    arg_keys = jax.random.split(jax.random.key(seed), 7)
    visibility = centred(arg_keys[0], (2, N_CHANNEL, BLOCKS, 2 * CHB, BV), 1.0, 6.0, ((0, 2), (1, 4), (2, 4)))
    kernel = centred(arg_keys[1], (2, N_CHANNEL, BLOCKS, BV, PIX), BV ** -0.5, 0.5, ((0, 2), (1, 4), (2, 4)))
    block_tile = draw_block_tile(jax.random.fold_in(arg_keys[6], 71), 0)
    block_chan = set_ends(jax.random.randint(arg_keys[3], (2, N_CHANNEL, BLOCKS), 0, CH_DEV - CHB + 1), jax.random.fold_in(arg_keys[3], 1), 0, CH_DEV - CHB).astype(jnp.int32)
    tile_owner = draw_tile_owner(jax.random.fold_in(arg_keys[6], 71), 0)
    inv_cov = draw_inv_cov(jax.random.fold_in(arg_keys[6], 71), 0)
    return dict(visibility=visibility, kernel=kernel, block_tile=block_tile, block_chan=block_chan, tile_owner=tile_owner, inv_cov=inv_cov)


def delay_table(count):
    indices = jnp.arange(count, dtype=jnp.int32)
    phase_int = (indices[:, None] * indices[None, :]) % count
    angles = phase_int.astype(jnp.float32) * (2.0 * math.pi / count)
    return jnp.concatenate([jnp.cos(angles), jnp.sin(angles)], axis=0).astype(jnp.bfloat16)


def block_terms(operand_pair):
    samples, weights = operand_pair
    return jnp.einsum("bkv,bvp->bkp", samples.astype(jnp.float32), weights.astype(jnp.float32)).astype(jnp.bfloat16)


def reference(visibility, kernel, block_tile, block_chan, tile_owner, inv_cov):
    indices = jnp.arange(TILES, dtype=jnp.int32)
    same_owner = (tile_owner[:, None] == tile_owner[None, :]) & (indices[:, None] < indices[None, :])
    tile_slot = jnp.sum(same_owner.astype(jnp.int32), axis=0).astype(jnp.int32)
    tile_cell = (tile_owner * TILE_DEV + tile_slot) * PIX
    chan_offsets = jnp.arange(CHB, dtype=jnp.int32)
    pix_offsets = jnp.arange(PIX, dtype=jnp.int32)
    group_base = jnp.arange(N_CHANNEL, dtype=jnp.int32)[:, None] * CH_DEV
    all_grids = []
    for parity in range(2):
        partials = lax.map(block_terms, (visibility[parity], kernel[parity]))
        row_index = (group_base + block_chan[parity])[..., None] + chan_offsets
        col_index = tile_cell[block_tile[parity]][..., None] + pix_offsets
        values = jnp.moveaxis(partials.reshape(N_CHANNEL, BLOCKS, 2, CHB, PIX), 2, 0).astype(jnp.float32)
        gridded = jnp.zeros((2, NCH, CELLS), jnp.float32).at[:, row_index[..., None], col_index[..., None, :]].add(values)
        all_grids.append(gridded.astype(jnp.bfloat16))
    all_grids = jnp.stack(all_grids)
    dft_table = delay_table(NCH).astype(jnp.float32)
    cov_wide = inv_cov.astype(jnp.float32)
    block_cells = math.gcd(CELLS, 2048)
    block_count = CELLS // block_cells

    def spectra(block_index):
        piece = lax.dynamic_slice_in_dim(all_grids, block_index * block_cells, block_cells, 3).astype(jnp.float32)
        weighted = jnp.einsum("ij,prjc->pric", cov_wide, piece).astype(jnp.bfloat16)
        weighted = lax.optimization_barrier(weighted).astype(jnp.float32)
        projected = jnp.einsum("ij,prjc->pric", dft_table, weighted)
        spec_real = projected[:, 0, :NCH] + projected[:, 1, NCH:]
        spec_imag = projected[:, 1, :NCH] - projected[:, 0, NCH:]
        cross_power = (spec_real[0] * spec_real[1] + spec_imag[0] * spec_imag[1]) / NCH
        real_gap = spec_real[0] - spec_real[1]
        imag_gap = spec_imag[0] - spec_imag[1]
        diff_power = (real_gap * real_gap + imag_gap * imag_gap) / NCH
        return cross_power, diff_power

    cross_blocks, diff_blocks = lax.map(spectra, jnp.arange(block_count, dtype=jnp.int32))
    cross_power = jnp.transpose(cross_blocks, (1, 0, 2)).reshape(NCH, CELLS)
    diff_power = jnp.transpose(diff_blocks, (1, 0, 2)).reshape(NCH, CELLS)
    return cross_power, diff_power
```

```python
import functools
import math

import jax
import jax.numpy as jnp
import ml_dtypes
import numpy as np
from jax import lax
from jax.experimental import pallas as pl
from jax.experimental.pallas import tpu as pltpu
from jax.sharding import PartitionSpec as P

MESH = pl.DeviceIdType.MESH


def half_table(count):
    half = count // 2
    phase = np.arange(half + 1)[:, None] * np.arange(count)[None, :] % count
    angles = phase.astype(np.float64) * (2.0 * math.pi / count)
    rows = np.concatenate([np.cos(angles[:half]), np.cos(angles[half:]), np.sin(angles[1:half])])
    return (rows.astype(np.float32).astype(ml_dtypes.bfloat16).astype(np.float32) / count).astype(
        ml_dtypes.bfloat16
    )


def pack_kernel(n_ch, slots, group_tiles, channels, tile, chan, owner, vis, ker, out, meta, slot_of, own_count, dest_count):
    blocks = vis.shape[0]
    dests = meta.shape[0]
    chan_base = lax.axis_index("channel") * (channels // n_ch)
    for index in range(own_count.shape[0]):
        own_count[index] = 0

    def clear(dest, _):
        dest_count[dest] = 0
        for rank in range(slots):
            meta[dest, 0, rank] = -1
        return 0

    lax.fori_loop(0, dests, clear, 0)

    def number(index, _):
        holder = owner[index]
        place = own_count[holder]
        slot_of[index] = place
        own_count[holder] = place + 1
        return 0

    lax.fori_loop(0, owner.shape[0], number, 0, unroll=8)
    for block in range(blocks):
        where = tile[block]
        place = slot_of[where]
        dest = owner[where] * n_ch + place // group_tiles
        rank = dest_count[dest]
        dest_count[dest] = rank + 1
        meta[dest, 0, rank] = place * channels + chan_base + chan[block]
        out[dest, rank] = jnp.dot(vis[block], ker[block], preferred_element_type=jnp.float32).astype(out.dtype)


def exchange_kernel(n_uv, n_ch, data, meta, got, got_meta, keep_sem, send_sem, recv_sem, fsend_sem, frecv_sem):
    dests = n_uv * n_ch
    u, c, p = lax.axis_index("uv"), lax.axis_index("channel"), lax.axis_index("parity")
    me = u * n_ch + c
    partner = (u, c, 1 - p)

    def peer(step):
        dest = lax.rem(me + step, dests)
        return dest, (lax.div(dest, n_ch), lax.rem(dest, n_ch), p)

    barrier = pltpu.get_barrier_semaphore()
    pl.semaphore_signal(barrier, inc=1, device_id=partner, device_id_type=MESH)

    def greet(step, _):
        pl.semaphore_signal(barrier, inc=1, device_id=peer(step)[1], device_id_type=MESH)
        return 0

    lax.fori_loop(1, dests, greet, 0)
    pl.semaphore_wait(barrier, dests)

    def copies(step, source, landing, sends, recvs, device):
        return [
            pltpu.make_async_remote_copy(
                src_ref=values,
                dst_ref=target,
                send_sem=sends.at[kind, step],
                recv_sem=recvs.at[kind, step],
                device_id=device,
                device_id_type=MESH,
            )
            for kind, (values, target) in enumerate(zip(source, landing))
        ]

    def outward(step):
        dest, device = peer(step)
        return copies(
            step, (data.at[dest], meta.at[dest]), (got.at[p, me], got_meta.at[p, me]), send_sem, recv_sem, device
        )

    def onward(step):
        origin = lax.rem(me + dests - step, dests)
        held = (got.at[p, origin], got_meta.at[p, origin])
        return copies(step, held, held, fsend_sem, frecv_sem, partner)

    def first_send(step, _):
        for copy in outward(step):
            copy.start()
        return 0

    lax.fori_loop(1, dests, first_send, 0)
    kept = [
        pltpu.make_async_copy(data.at[me], got.at[p, me], keep_sem.at[0]),
        pltpu.make_async_copy(meta.at[me], got_meta.at[p, me], keep_sem.at[1]),
    ]
    for copy in kept:
        copy.start()
    for copy in kept:
        copy.wait()
    for copy in onward(0):
        copy.start()

    def forward(step, _):
        for copy in outward(step):
            copy.wait_recv()
        for copy in onward(step):
            copy.start()
        return 0

    lax.fori_loop(1, dests, forward, 0)

    def finish(step, _):
        for copy in outward(step):
            copy.wait_send()
        return 0

    lax.fori_loop(1, dests, finish, 0)

    def close(step, _):
        for copy in onward(step):
            copy.wait()
        return 0

    lax.fori_loop(0, dests, close, 0)


def power_kernel(n_ch, slots, dests, tiles, scale, meta, got, mix, cross, diff, acc, grid, high, count, listing):
    step = pl.program_id(0)
    channels = mix.shape[0]
    half = channels // 2
    pixels = cross.shape[1]
    width = got.shape[1] // 2
    capacity = dests * slots
    window = 2 * width

    @pl.when(step == 0)
    def _():
        acc[...] = jnp.zeros_like(acc)
        grid[...] = jnp.zeros_like(grid)
        base = (lax.axis_index("channel") * 2 + lax.axis_index("parity")) * tiles
        for index in range(2 * tiles):
            count[index] = 0
        for parity in range(2):

            def scan(origin, _):
                for rank in range(slots):
                    entry = meta[parity, origin, 0, rank]
                    local = lax.div(entry, channels) - base

                    @pl.when((entry >= 0) & (local >= 0) & (local < tiles))
                    def _():
                        row = local * 2 + parity
                        at = count[row]
                        count[row] = at + 1
                        place = (parity * dests + origin) * slots + rank
                        listing[row * capacity + at] = place * channels + lax.rem(entry, channels)

                return 0

            lax.fori_loop(0, dests, scan, 0)

    def where(parity, index):
        entry = listing[(step * 2 + parity) * capacity + index]
        first = lax.rem(entry, channels)
        aligned = jnp.minimum(lax.div(first, width) * width, channels - window)
        aligned = pl.multiple_of(aligned, width)
        return lax.div(entry, channels), first - aligned, aligned

    for parity in range(2):
        total = count[step * 2 + parity]

        def add(index, _):
            place, shift, aligned = where(parity, index)
            block = got[place].astype(jnp.float32) * scale
            filler = jnp.zeros((window - width, pixels), jnp.float32)
            for part in range(2):
                moved = pltpu.roll(
                    jnp.concatenate([block[part * width : (part + 1) * width], filler], axis=0), shift, 0
                )
                columns = slice(part * pixels, (part + 1) * pixels)
                acc[pl.ds(aligned, window), columns] += moved
            return 0

        lax.fori_loop(0, total, add, 0)

        def keep(index, _):
            _, _, aligned = where(parity, index)
            columns = slice(2 * parity * pixels, 2 * (parity + 1) * pixels)
            grid[pl.ds(aligned, window), columns] = acc[pl.ds(aligned, window), :].astype(grid.dtype)
            return 0

        lax.fori_loop(0, total, keep, 0)

        def wipe(index, _):
            _, _, aligned = where(parity, index)
            acc[pl.ds(aligned, window), :] = jnp.zeros((window, 2 * pixels), jnp.float32)
            return 0

        lax.fori_loop(0, total, wipe, 0)

    rows = math.gcd(half, 128)

    def powers(spec):
        even_real, even_imag, odd_real, odd_imag = spec
        real_gap, imag_gap = even_real - odd_real, even_imag - odd_imag
        return even_real * odd_real + even_imag * odd_imag, real_gap * real_gap + imag_gap * imag_gap

    for start in range(0, half, rows):
        cosine = jnp.dot(mix[start : start + rows, :], grid[...], preferred_element_type=jnp.float32)
        sine = jnp.dot(mix[half + start : half + start + rows, :], grid[...], preferred_element_type=jnp.float32)
        cos_parts = [cosine[:, k * pixels : (k + 1) * pixels] for k in range(4)]
        sin_parts = [sine[:, k * pixels : (k + 1) * pixels] for k in range(4)]
        if start == 0:
            ends = powers([part[:8] for part in sin_parts])
            high[0, half : half + 8, :] = ends[0]
            high[1, half : half + 8, :] = ends[1]
            first = lax.broadcasted_iota(jnp.int32, (rows, pixels), 0) == 0
            sin_parts = [jnp.where(first, 0.0, part) for part in sin_parts]
        low, top = [], []
        for parity in range(2):
            cr, ci = cos_parts[2 * parity : 2 * parity + 2]
            sr, si = sin_parts[2 * parity : 2 * parity + 2]
            low += [cr + si, ci - sr]
            top += [cr - si, ci + sr]
        low_powers = powers(low)
        cross[start : start + rows, :] = low_powers[0]
        diff[start : start + rows, :] = low_powers[1]
        top_powers = powers(top)
        high[0, start : start + rows, :] = top_powers[0]
        high[1, start : start + rows, :] = top_powers[1]

    backwards = 7 - lax.broadcasted_iota(jnp.int32, (8, pixels), 0)
    for row in range(0, half, 8):
        for which, target in enumerate((cross, diff)):
            piece = high[which, half - row - 7 : half - row + 1, :]
            target[half + row : half + row + 8, :] = jnp.take_along_axis(piece, backwards, axis=0)

    for parity in range(2):

        def clean(index, _):
            _, _, aligned = where(parity, index)
            columns = slice(2 * parity * pixels, 2 * (parity + 1) * pixels)
            grid[pl.ds(aligned, window), columns] = jnp.zeros((window, 2 * pixels), grid.dtype)
            return 0

        lax.fori_loop(0, count[step * 2 + parity], clean, 0)


def on_device(visibility, kernel, block_tile, block_chan, tile_owner, inv_cov):
    n_uv = lax.axis_size("uv")
    n_ch = lax.axis_size("channel")
    n_par = lax.axis_size("parity")
    samples = visibility[0, 0]
    weights = kernel[0, 0]
    blocks, doubled, _ = samples.shape
    pixels = weights.shape[2]
    channels = inv_cov.shape[0]
    tile_total = tile_owner.shape[0]
    group_tiles = tile_total // n_uv // n_ch
    out_tiles = group_tiles // n_par
    dests = n_uv * n_ch
    slots = max(1, 2 * blocks // dests)
    smem = pl.BlockSpec(memory_space=pltpu.SMEM)
    vmem = pl.BlockSpec(memory_space=pltpu.VMEM)
    anywhere = pl.BlockSpec(memory_space=pl.ANY)

    mix = jnp.dot(half_table(channels), inv_cov, preferred_element_type=jnp.float32).astype(jnp.bfloat16)

    outgoing, meta = pl.pallas_call(
        functools.partial(pack_kernel, n_ch, slots, group_tiles, channels),
        out_shape=(
            jax.ShapeDtypeStruct((dests, slots, doubled, pixels), jnp.bfloat16),
            jax.ShapeDtypeStruct((dests, 1, 128), jnp.int32),
        ),
        in_specs=[smem, smem, smem, vmem, vmem],
        out_specs=(vmem, smem),
        scratch_shapes=[
            pltpu.SMEM((tile_total,), jnp.int32),
            pltpu.SMEM((n_uv,), jnp.int32),
            pltpu.SMEM((dests,), jnp.int32),
        ],
        compiler_params=pltpu.CompilerParams(vmem_limit_bytes=32 << 20),
        name="pack_terms",
    )(block_tile[0, 0], block_chan[0, 0], tile_owner, samples, weights)

    got, got_meta = pl.pallas_call(
        functools.partial(exchange_kernel, n_uv, n_ch),
        out_shape=(
            jax.ShapeDtypeStruct((2, dests, slots, doubled, pixels), jnp.bfloat16),
            jax.ShapeDtypeStruct((2, dests, 1, 128), jnp.int32),
        ),
        in_specs=[vmem, vmem],
        out_specs=(vmem, vmem),
        scratch_shapes=[
            pltpu.SemaphoreType.DMA((2,)),
            pltpu.SemaphoreType.DMA((2, dests)),
            pltpu.SemaphoreType.DMA((2, dests)),
            pltpu.SemaphoreType.DMA((2, dests)),
            pltpu.SemaphoreType.DMA((2, dests)),
        ],
        compiler_params=pltpu.CompilerParams(
            collective_id=0, has_side_effects=True, vmem_limit_bytes=32 << 20
        ),
        name="exchange_terms",
    )(outgoing, meta)

    area = pl.BlockSpec((channels, pixels), lambda t: (0, t))
    return pl.pallas_call(
        functools.partial(power_kernel, n_ch, slots, dests, out_tiles, math.sqrt(channels)),
        grid=(out_tiles,),
        out_shape=(jax.ShapeDtypeStruct((channels, out_tiles * pixels), jnp.float32),) * 2,
        in_specs=[smem, vmem, vmem],
        out_specs=(area, area),
        scratch_shapes=[
            pltpu.VMEM((channels, 2 * pixels), jnp.float32),
            pltpu.VMEM((channels, 4 * pixels), jnp.bfloat16),
            pltpu.VMEM((2, channels // 2 + 8, pixels), jnp.float32),
            pltpu.SMEM((2 * out_tiles,), jnp.int32),
            pltpu.SMEM((2 * out_tiles * dests * slots,), jnp.int32),
        ],
        compiler_params=pltpu.CompilerParams(vmem_limit_bytes=48 << 20),
        name="power_spectra",
    )(got_meta, got.reshape(2 * dests * slots, doubled, pixels), mix)


def solution(mesh):
    placed = (
        P("parity", "channel", "uv", None, None),
        P("parity", "channel", "uv", None, None),
        P("parity", "channel", "uv"),
        P("parity", "channel", "uv"),
        P(),
        P(),
    )
    return jax.shard_map(
        on_device,
        mesh=mesh,
        in_specs=placed,
        out_specs=(P(None, ("uv", "channel", "parity")), P(None, ("uv", "channel", "parity"))),
        check_vma=False,
    )
```

```python
import functools
import math

import jax
import jax.numpy as jnp
import ml_dtypes
import numpy as np
from jax import lax
from jax.experimental import pallas as pl
from jax.experimental.pallas import tpu as pltpu
from jax.sharding import PartitionSpec as P

MESH = pl.DeviceIdType.MESH


def half_table(count):
    half = count // 2
    phase = np.arange(half + 1)[:, None] * np.arange(count)[None, :] % count
    angles = phase.astype(np.float64) * (2.0 * math.pi / count)
    run = math.gcd(half, 256)
    pair = np.stack([np.cos(angles[:half]), np.concatenate([np.cos(angles[half:]), np.sin(angles[1:half])])])
    rows = pair.reshape(2, half // run, run, count).swapaxes(0, 1).reshape(count, count)
    return rows.astype(np.float32).astype(ml_dtypes.bfloat16).astype(np.float32) / np.float32(count)


def pack_kernel(
    n_ch, slots, group_tiles, channels, tile_in, chan_in, owner_in, vis_in, ker_in, out, meta,
    tile, chan, owner, vis, ker, slot_of, own_count, dest_count, lines, sems,
):
    blocks = vis.shape[0]
    dests = meta.shape[0]
    share = blocks // lines
    pieces = [pl.ds(index * share, share) for index in range(lines)]
    routes = [
        pltpu.make_async_copy(source, target, sems.at[index])
        for index, (source, target) in enumerate(((owner_in, owner), (tile_in, tile), (chan_in, chan)))
    ]
    loads = [pltpu.make_async_copy(vis_in, vis, sems.at[3])]
    loads += [
        pltpu.make_async_copy(ker_in.at[piece], ker.at[piece], sems.at[4 + index])
        for index, piece in enumerate(pieces)
    ]
    for copy in routes + loads:
        copy.start()
    chan_base = lax.axis_index("channel") * (channels // n_ch)
    for index in range(own_count.shape[0]):
        own_count[index] = 0

    def clear(dest, _):
        dest_count[dest] = 0
        for rank in range(slots):
            meta[dest, 0, rank] = -1
            meta[dest, 0, slots + rank] = 0
        return 0

    lax.fori_loop(0, dests, clear, 0)
    for copy in routes:
        copy.wait()

    def number(index, _):
        holder = owner[index]
        place = own_count[holder]
        slot_of[index] = place
        own_count[holder] = place + 1
        return 0

    lax.fori_loop(0, owner.shape[0], number, 0, unroll=8)
    loads[0].wait()
    for block in range(blocks):
        if block % share == 0:
            loads[1 + block // share].wait()
        where = tile[block]
        place = slot_of[where]
        dest = owner[where] * n_ch + place // group_tiles
        rank = dest_count[dest]
        dest_count[dest] = rank + 1
        meta[dest, 0, rank] = place
        meta[dest, 0, slots + rank] = chan_base + chan[block]
        out[dest, rank] = jnp.dot(vis[block], ker[block], preferred_element_type=jnp.float32).astype(out.dtype)


def exchange_kernel(
    n_uv, n_ch, data, meta, table_in, cov, got, got_meta, mix_out, table, mix, keep_sem, send_sem, recv_sem, fsend_sem, frecv_sem
):
    dests = n_uv * n_ch
    ahead = min(6, dests)
    u, c, p = lax.axis_index("uv"), lax.axis_index("channel"), lax.axis_index("parity")
    me = u * n_ch + c
    partner = (u, c, 1 - p)

    table_copy = pltpu.make_async_copy(table_in, table, keep_sem.at[2])
    table_copy.start()

    def peer(step):
        dest = lax.rem(me + step, dests)
        return dest, (lax.div(dest, n_ch), lax.rem(dest, n_ch), p)

    barrier = pltpu.get_barrier_semaphore()
    pl.semaphore_signal(barrier, inc=1, device_id=partner, device_id_type=MESH)

    def greet(step, _):
        pl.semaphore_signal(barrier, inc=1, device_id=peer(step)[1], device_id_type=MESH)
        return 0

    lax.fori_loop(1, dests, greet, 0)
    pl.semaphore_wait(barrier, dests)

    def copies(step, source, landing, sends, recvs, device):
        return [
            pltpu.make_async_remote_copy(
                src_ref=values,
                dst_ref=target,
                send_sem=sends.at[kind, step],
                recv_sem=recvs.at[kind, step],
                device_id=device,
                device_id_type=MESH,
            )
            for kind, (values, target) in enumerate(zip(source, landing))
        ]

    def outward(step):
        dest, device = peer(step)
        return copies(
            step, (data.at[dest], meta.at[dest]), (got.at[p, me], got_meta.at[p, me]), send_sem, recv_sem, device
        )

    def onward(step):
        origin = lax.rem(me + dests - step, dests)
        held = (got.at[p, origin], got_meta.at[p, origin])
        return copies(step, held, held, fsend_sem, frecv_sem, partner)

    def first_send(step, _):
        for copy in outward(step):
            copy.start()
        return 0

    lax.fori_loop(1, ahead, first_send, 0)
    kept = [
        pltpu.make_async_copy(data.at[me], got.at[p, me], keep_sem.at[0]),
        pltpu.make_async_copy(meta.at[me], got_meta.at[p, me], keep_sem.at[1]),
    ]
    for copy in kept:
        copy.start()
    for copy in kept:
        copy.wait()
    for copy in onward(0):
        copy.start()

    rows = math.gcd(mix.shape[0], 256)

    def join(index, _):
        part = pl.ds(pl.multiple_of(index * rows, rows), rows)
        mix[part, :] = jnp.dot(table[part, :].astype(cov.dtype), cov[...], preferred_element_type=jnp.float32).astype(mix.dtype)
        return 0

    table_copy.wait()
    lax.fori_loop(0, mix.shape[0] // rows, join, 0)
    mix_copy = pltpu.make_async_copy(mix, mix_out, keep_sem.at[3])
    mix_copy.start()

    def forward(step, more):
        for copy in outward(step):
            copy.wait_recv()
        for copy in onward(step):
            copy.start()
        if more:
            first_send(step + ahead - 1, 0)

    def forward_more(step, _):
        forward(step, True)
        return 0

    def forward_last(step, _):
        forward(step, False)
        return 0

    lax.fori_loop(1, dests - ahead + 1, forward_more, 0)
    lax.fori_loop(dests - ahead + 1, dests, forward_last, 0)

    mix_copy.wait()

    def finish(step, _):
        for copy in outward(step):
            copy.wait_send()
        return 0

    lax.fori_loop(1, dests, finish, 0)

    def close(step, _):
        for copy in onward(step):
            copy.wait()
        return 0

    lax.fori_loop(0, dests, close, 0)


def power_kernel(
    n_ch, slots, dests, tiles, scale, meta, got, mix, cross, diff, acc, grid, high, count, place_of, first_of
):
    step = pl.program_id(0)
    channels = mix.shape[0]
    half = channels // 2
    pixels = cross.shape[1]
    width = got.shape[1] // 2
    capacity = dests * slots
    window = 2 * width

    @pl.when(step == 0)
    def _():
        acc[...] = jnp.zeros_like(acc)
        grid[...] = jnp.zeros_like(grid)
        base = (lax.axis_index("channel") * 2 + lax.axis_index("parity")) * tiles
        for index in range(2 * tiles + 1):
            count[index] = 0

        def scan(origin, _):
            for parity in range(2):
                for rank in range(slots):
                    slot = meta[parity, origin, 0, rank]
                    local = slot - base
                    mine = (slot >= 0) & (local >= 0) & (local < tiles)
                    row = jnp.where(mine, local * 2 + parity, 2 * tiles)
                    at = count[row]
                    count[row] = at + 1
                    spot = jnp.where(mine, row * capacity + at, 2 * tiles * capacity)
                    place_of[spot] = (parity * dests + origin) * slots + rank
                    first_of[spot] = meta[parity, origin, 0, slots + rank]
            return 0

        lax.fori_loop(0, dests, scan, 0)

    def align(spot):
        first = first_of[spot]
        aligned = jnp.minimum(first - lax.rem(first, width), channels - window)
        return first - aligned, pl.multiple_of(aligned, width)

    for parity in range(2):
        listed = (step * 2 + parity) * capacity

        def add(index, _):
            shift, aligned = align(listed + index)
            block = got[place_of[listed + index]].astype(jnp.float32) * scale
            filler = jnp.zeros((window - width, pixels), jnp.float32)
            for part in range(2):
                moved = pltpu.roll(
                    jnp.concatenate([block[part * width : (part + 1) * width], filler], axis=0), shift, 0
                )
                columns = slice((2 * parity + part) * pixels, (2 * parity + part + 1) * pixels)
                total = acc[pl.ds(aligned, window), columns] + moved
                acc[pl.ds(aligned, window), columns] = total
                grid[pl.ds(aligned, window), columns] = total.astype(grid.dtype)
            return 0

        lax.fori_loop(0, count[step * 2 + parity], add, 0)

    rows = math.gcd(half, 256)

    def powers(spec):
        even_real, even_imag, odd_real, odd_imag = spec
        real_gap, imag_gap = even_real - odd_real, even_imag - odd_imag
        return even_real * odd_real + even_imag * odd_imag, real_gap * real_gap + imag_gap * imag_gap

    for start in range(0, half, rows):
        both = jnp.dot(mix[2 * start : 2 * start + 2 * rows, :], grid[...], preferred_element_type=jnp.float32)
        cosine, sine = both[:rows], both[rows:]
        cos_parts = [cosine[:, k * pixels : (k + 1) * pixels] for k in range(4)]
        sin_parts = [sine[:, k * pixels : (k + 1) * pixels] for k in range(4)]
        if start == 0:
            ends = powers([part[:8] for part in sin_parts])
            high[0, half : half + 8, :] = ends[0]
            high[1, half : half + 8, :] = ends[1]
            first = lax.broadcasted_iota(jnp.int32, (rows, pixels), 0) == 0
            sin_parts = [jnp.where(first, 0.0, part) for part in sin_parts]
        low, top = [], []
        for parity in range(2):
            cr, ci = cos_parts[2 * parity : 2 * parity + 2]
            sr, si = sin_parts[2 * parity : 2 * parity + 2]
            low += [cr + si, ci - sr]
            top += [cr - si, ci + sr]
        low_powers = powers(low)
        cross[start : start + rows, :] = low_powers[0]
        diff[start : start + rows, :] = low_powers[1]
        top_powers = powers(top)
        high[0, start : start + rows, :] = top_powers[0]
        high[1, start : start + rows, :] = top_powers[1]

    backwards = 7 - lax.broadcasted_iota(jnp.int32, (8, pixels), 0)
    for row in range(0, half, 8):
        for which, target in enumerate((cross, diff)):
            piece = high[which, half - row - 7 : half - row + 1, :]
            target[half + row : half + row + 8, :] = jnp.take_along_axis(piece, backwards, axis=0)

    for parity in range(2):

        listed = (step * 2 + parity) * capacity

        def clean(index, _):
            _, aligned = align(listed + index)
            columns = slice(2 * parity * pixels, 2 * (parity + 1) * pixels)
            acc[pl.ds(aligned, window), columns] = jnp.zeros((window, 2 * pixels), acc.dtype)
            grid[pl.ds(aligned, window), columns] = jnp.zeros((window, 2 * pixels), grid.dtype)
            return 0

        lax.fori_loop(0, count[step * 2 + parity], clean, 0)


def on_device(visibility, kernel, block_tile, block_chan, tile_owner, inv_cov):
    n_uv = lax.axis_size("uv")
    n_ch = lax.axis_size("channel")
    n_par = lax.axis_size("parity")
    samples = visibility[0, 0]
    weights = kernel[0, 0]
    blocks, doubled, _ = samples.shape
    pixels = weights.shape[2]
    channels = inv_cov.shape[0]
    tile_total = tile_owner.shape[0]
    group_tiles = tile_total // n_uv // n_ch
    out_tiles = group_tiles // n_par
    dests = n_uv * n_ch
    slots = max(1, 2 * blocks // dests)
    smem = pl.BlockSpec(memory_space=pltpu.SMEM)
    vmem = pl.BlockSpec(memory_space=pltpu.VMEM)
    anywhere = pl.BlockSpec(memory_space=pl.ANY)
    lines = math.gcd(blocks, 4)

    outgoing, meta = pl.pallas_call(
        lambda *refs: pack_kernel(n_ch, slots, group_tiles, channels, *refs[:-1], lines, refs[-1]),
        out_shape=(
            jax.ShapeDtypeStruct((dests, slots, doubled, pixels), jnp.bfloat16),
            jax.ShapeDtypeStruct((dests, 1, 128), jnp.int32),
        ),
        in_specs=[pl.BlockSpec(memory_space=pltpu.HBM)] * 5,
        out_specs=(vmem, smem),
        scratch_shapes=[
            pltpu.SMEM((blocks,), jnp.int32),
            pltpu.SMEM((blocks,), jnp.int32),
            pltpu.SMEM((tile_total,), jnp.int32),
            pltpu.VMEM(samples.shape, samples.dtype),
            pltpu.VMEM(weights.shape, weights.dtype),
            pltpu.SMEM((tile_total,), jnp.int32),
            pltpu.SMEM((n_uv,), jnp.int32),
            pltpu.SMEM((dests,), jnp.int32),
            pltpu.SemaphoreType.DMA((4 + lines,)),
        ],
        compiler_params=pltpu.CompilerParams(vmem_limit_bytes=60 << 20),
        name="pack_terms",
    )(block_tile[0, 0], block_chan[0, 0], tile_owner, samples, weights)

    got, got_meta, mix = pl.pallas_call(
        functools.partial(exchange_kernel, n_uv, n_ch),
        out_shape=(
            jax.ShapeDtypeStruct((2, dests, slots, doubled, pixels), jnp.bfloat16),
            jax.ShapeDtypeStruct((2, dests, 1, 128), jnp.int32),
            jax.ShapeDtypeStruct((channels, channels), jnp.bfloat16),
        ),
        in_specs=[anywhere, anywhere, anywhere, vmem],
        out_specs=(anywhere, anywhere, anywhere),
        scratch_shapes=[
            pltpu.VMEM((channels, channels), jnp.float32),
            pltpu.VMEM((channels, channels), jnp.bfloat16),
            pltpu.SemaphoreType.DMA((4,)),
            pltpu.SemaphoreType.DMA((2, dests)),
            pltpu.SemaphoreType.DMA((2, dests)),
            pltpu.SemaphoreType.DMA((2, dests)),
            pltpu.SemaphoreType.DMA((2, dests)),
        ],
        compiler_params=pltpu.CompilerParams(
            collective_id=0, has_side_effects=True, vmem_limit_bytes=57 << 20
        ),
        name="exchange_terms",
    )(outgoing, meta, half_table(channels), inv_cov)

    area = pl.BlockSpec((channels, pixels), lambda t: (0, t))
    return pl.pallas_call(
        functools.partial(power_kernel, n_ch, slots, dests, out_tiles, math.sqrt(channels)),
        grid=(out_tiles,),
        out_shape=(jax.ShapeDtypeStruct((channels, out_tiles * pixels), jnp.float32),) * 2,
        in_specs=[smem, vmem, vmem],
        out_specs=(area, area),
        scratch_shapes=[
            pltpu.VMEM((channels, 4 * pixels), jnp.float32),
            pltpu.VMEM((channels, 4 * pixels), jnp.bfloat16),
            pltpu.VMEM((2, channels // 2 + 8, pixels), jnp.float32),
            pltpu.SMEM((2 * out_tiles + 1,), jnp.int32),
            pltpu.SMEM((2 * out_tiles * dests * slots + 1,), jnp.int32),
            pltpu.SMEM((2 * out_tiles * dests * slots + 1,), jnp.int32),
        ],
        compiler_params=pltpu.CompilerParams(vmem_limit_bytes=60 << 20),
        name="power_spectra",
    )(got_meta, got.reshape(2 * dests * slots, doubled, pixels), mix)


def solution(mesh):
    placed = (
        P("parity", "channel", "uv", None, None),
        P("parity", "channel", "uv", None, None),
        P("parity", "channel", "uv"),
        P("parity", "channel", "uv"),
        P(),
        P(),
    )
    return jax.shard_map(
        on_device,
        mesh=mesh,
        in_specs=placed,
        out_specs=(P(None, ("uv", "channel", "parity")), P(None, ("uv", "channel", "parity"))),
        check_vma=False,
    )
```

```python
import functools
import math

import jax
import jax.numpy as jnp
import ml_dtypes
import numpy as np
from jax import lax
from jax.experimental import pallas as pl
from jax.experimental.pallas import tpu as pltpu
from jax.sharding import PartitionSpec as P

MESH = pl.DeviceIdType.MESH


def half_table(count):
    half = count // 2
    phase = np.arange(half + 1)[:, None] * np.arange(count)[None, :] % count
    angles = phase.astype(np.float64) * (2.0 * math.pi / count)
    run = math.gcd(half, 256)
    pair = np.stack([np.cos(angles[:half]), np.concatenate([np.cos(angles[half:]), np.sin(angles[1:half])])])
    rows = pair.reshape(2, half // run, run, count).swapaxes(0, 1).reshape(count, count)
    return rows.astype(np.float32).astype(ml_dtypes.bfloat16).astype(np.float32) / np.float32(count)


def pack_kernel(
    n_ch, slots, group_tiles, channels, tile_in, chan_in, owner_in, vis_in, ker_in, out, meta,
    tile, chan, owner, vis, ker, slot_of, own_count, dest_count, lines, sems,
):
    blocks = vis.shape[0]
    dests = meta.shape[0]
    share = blocks // lines
    pieces = [pl.ds(index * share, share) for index in range(lines)]
    routes = [
        pltpu.make_async_copy(source, target, sems.at[index])
        for index, (source, target) in enumerate(((owner_in, owner), (tile_in, tile), (chan_in, chan)))
    ]
    loads = [pltpu.make_async_copy(vis_in, vis, sems.at[3])]
    loads += [
        pltpu.make_async_copy(ker_in.at[piece], ker.at[piece], sems.at[4 + index])
        for index, piece in enumerate(pieces)
    ]
    for copy in routes + loads:
        copy.start()
    chan_base = lax.axis_index("channel") * (channels // n_ch)
    for index in range(own_count.shape[0]):
        own_count[index] = 0

    def clear(dest, _):
        dest_count[dest] = 0
        for rank in range(slots):
            meta[dest, 0, rank] = -1
            meta[dest, 0, slots + rank] = 0
        return 0

    lax.fori_loop(0, dests, clear, 0)
    for copy in routes:
        copy.wait()

    def number(index, _):
        holder = owner[index]
        place = own_count[holder]
        slot_of[index] = place
        own_count[holder] = place + 1
        return 0

    lax.fori_loop(0, owner.shape[0], number, 0, unroll=8)
    loads[0].wait()
    for block in range(blocks):
        if block % share == 0:
            loads[1 + block // share].wait()
        where = tile[block]
        place = slot_of[where]
        dest = owner[where] * n_ch + place // group_tiles
        rank = dest_count[dest]
        dest_count[dest] = rank + 1
        meta[dest, 0, rank] = place
        meta[dest, 0, slots + rank] = chan_base + chan[block]
        out[dest, rank] = jnp.dot(vis[block], ker[block], preferred_element_type=jnp.float32).astype(out.dtype)


def exchange_kernel(
    n_uv, n_ch, data, meta, table_in, cov, got, got_meta, mix_out, table, mix, keep_sem, send_sem, recv_sem, fsend_sem, frecv_sem
):
    dests = n_uv * n_ch
    ahead = min(6, dests)
    u, c, p = lax.axis_index("uv"), lax.axis_index("channel"), lax.axis_index("parity")
    me = u * n_ch + c
    partner = (u, c, 1 - p)

    table_copy = pltpu.make_async_copy(table_in, table, keep_sem.at[2])
    table_copy.start()

    turn = dests + (1 - 2 * lax.rem(u, 2))

    def peer(step):
        dest = lax.rem(me + lax.rem(turn, dests) * step, dests)
        return dest, (lax.div(dest, n_ch), lax.rem(dest, n_ch), p)

    barrier = pltpu.get_barrier_semaphore()
    pl.semaphore_signal(barrier, inc=1, device_id=partner, device_id_type=MESH)

    def greet(step, _):
        pl.semaphore_signal(barrier, inc=1, device_id=peer(step)[1], device_id_type=MESH)
        return 0

    lax.fori_loop(1, dests, greet, 0)
    pl.semaphore_wait(barrier, dests)

    def copies(send_at, recv_at, source, landing, sends, recvs, device):
        return [
            pltpu.make_async_remote_copy(
                src_ref=values,
                dst_ref=target,
                send_sem=sends.at[kind, send_at],
                recv_sem=recvs.at[kind, recv_at],
                device_id=device,
                device_id_type=MESH,
            )
            for kind, (values, target) in enumerate(zip(source, landing))
        ]

    def outward(step):
        dest, device = peer(step)
        landing = (got.at[p, me], got_meta.at[p, me])
        return copies(dest, me, (data.at[dest], meta.at[dest]), landing, send_sem, recv_sem, device)

    def inward(origin):
        landing = (got.at[p, origin], got_meta.at[p, origin])
        return copies(origin, origin, (data.at[origin], meta.at[origin]), landing, send_sem, recv_sem, partner)

    def onward(origin):
        held = (got.at[p, origin], got_meta.at[p, origin])
        return copies(origin, origin, held, held, fsend_sem, frecv_sem, partner)

    def first_send(step, _):
        for copy in outward(step):
            copy.start()
        return 0

    lax.fori_loop(1, ahead, first_send, 0)
    kept = [
        pltpu.make_async_copy(data.at[me], got.at[p, me], keep_sem.at[0]),
        pltpu.make_async_copy(meta.at[me], got_meta.at[p, me], keep_sem.at[1]),
    ]
    for copy in kept:
        copy.start()
    for copy in kept:
        copy.wait()
    for copy in onward(me):
        copy.start()

    groups, channels, lanes = mix.shape
    rows = math.gcd(channels, 256)

    def join(index, _):
        part = pl.ds(pl.multiple_of(index * rows, rows), rows)
        joined = jnp.dot(table[part, :].astype(cov.dtype), cov[...], preferred_element_type=jnp.float32)
        for group in range(groups):
            mix[group, part, :] = joined[:, group * lanes : (group + 1) * lanes].astype(mix.dtype)
        return 0

    table_copy.wait()
    lax.fori_loop(0, channels // rows, join, 0)
    mix_copy = pltpu.make_async_copy(mix, mix_out, keep_sem.at[3])
    mix_copy.start()

    def forward(step, more):
        for side, shift in enumerate((dests - step, step)):
            origin = lax.rem(me + shift, dests)

            @pl.when(lax.rem(lax.div(origin, n_ch), 2) == side)
            def _():
                for copy in inward(origin):
                    copy.wait_recv()
                for copy in onward(origin):
                    copy.start()

        if more:
            first_send(step + ahead - 1, 0)

    def forward_more(step, _):
        forward(step, True)
        return 0

    def forward_last(step, _):
        forward(step, False)
        return 0

    lax.fori_loop(1, dests - ahead + 1, forward_more, 0)
    lax.fori_loop(dests - ahead + 1, dests, forward_last, 0)

    mix_copy.wait()

    def finish(step, _):
        for copy in outward(step):
            copy.wait_send()
        return 0

    lax.fori_loop(1, dests, finish, 0)

    def close(step, _):
        for copy in onward(step):
            copy.wait()
        return 0

    lax.fori_loop(0, dests, close, 0)


def power_kernel(
    n_ch, slots, dests, tiles, scale, meta, got, mix, cross, diff, acc, grid, high, count, place_of, first_of, spot_of, group_at
):
    step = pl.program_id(0)
    groups, channels, lanes = mix.shape
    half = channels // 2
    pixels = cross.shape[1]
    width = got.shape[1] // 2
    capacity = dests * slots
    assert lanes % width == 0

    @pl.when(step == 0)
    def _():
        acc[...] = jnp.zeros_like(acc)
        grid[...] = jnp.zeros_like(grid)
        base = (lax.axis_index("channel") * 2 + lax.axis_index("parity")) * tiles
        for index in range(2 * tiles + 1):
            count[index] = 0

        def scan(origin, _):
            for parity in range(2):
                for rank in range(slots):
                    slot = meta[parity, origin, 0, rank]
                    local = slot - base
                    mine = (slot >= 0) & (local >= 0) & (local < tiles)
                    row = jnp.where(mine, local * 2 + parity, 2 * tiles)
                    at = count[row]
                    count[row] = at + 1
                    spot = jnp.where(mine, row * capacity + at, 2 * tiles * capacity)
                    place_of[spot] = (parity * dests + origin) * slots + rank
                    first_of[spot] = meta[parity, origin, 0, slots + rank]
            return 0

        lax.fori_loop(0, dests, scan, 0)

    for group in range(groups):
        spot_of[group] = -1
        group_at[group] = 0

    def halves(entry):
        first = first_of[entry]
        shift = lax.rem(first, width)
        aligned = first - shift
        return shift, (aligned, jnp.where(shift > 0, aligned + width, aligned))

    used = jnp.int32(0)
    for parity in range(2):
        listed = (step * 2 + parity) * capacity

        def add(index, used):
            shift, starts = halves(listed + index)
            block = got[place_of[listed + index]].astype(jnp.float32) * scale
            filler = jnp.zeros((width, pixels), jnp.float32)
            moved = [
                pltpu.roll(jnp.concatenate([block[part * width : (part + 1) * width], filler], axis=0), shift, 0)
                for part in range(2)
            ]
            for side, begin in enumerate(starts):
                group = lax.div(begin, lanes)
                known = spot_of[group]
                spot = jnp.where(known < 0, used, known)
                used = jnp.where(known < 0, used + 1, used)
                spot_of[group] = spot
                group_at[spot] = group
                target = pl.ds(pl.multiple_of(spot * lanes + lax.rem(begin, lanes), width), width)
                for part in range(2):
                    columns = slice((2 * parity + part) * pixels, (2 * parity + part + 1) * pixels)
                    total = acc[target, columns] + moved[part][side * width : (side + 1) * width]
                    acc[target, columns] = total
                    grid[target, columns] = total.astype(grid.dtype)
            return used

        used = lax.fori_loop(0, count[step * 2 + parity], add, used)

    rows = math.gcd(half, 256)

    def powers(spec):
        even_real, even_imag, odd_real, odd_imag = spec
        real_gap, imag_gap = even_real - odd_real, even_imag - odd_imag
        return even_real * odd_real + even_imag * odd_imag, real_gap * real_gap + imag_gap * imag_gap

    def transform(amount):
        chosen = [group_at[index] for index in range(amount)]
        for start in range(0, half, rows):
            left = jnp.concatenate([mix[group, 2 * start : 2 * start + 2 * rows, :] for group in chosen], axis=1)
            both = jnp.dot(left, grid[: len(chosen) * lanes, :], preferred_element_type=jnp.float32)
            cosine, sine = both[:rows], both[rows:]
            cos_parts = [cosine[:, k * pixels : (k + 1) * pixels] for k in range(4)]
            sin_parts = [sine[:, k * pixels : (k + 1) * pixels] for k in range(4)]
            if start == 0:
                ends = powers([part[:8] for part in sin_parts])
                high[0, half : half + 8, :] = ends[0]
                high[1, half : half + 8, :] = ends[1]
                first = lax.broadcasted_iota(jnp.int32, (rows, pixels), 0) == 0
                sin_parts = [jnp.where(first, 0.0, part) for part in sin_parts]
            low, top = [], []
            for parity in range(2):
                cr, ci = cos_parts[2 * parity : 2 * parity + 2]
                sr, si = sin_parts[2 * parity : 2 * parity + 2]
                low += [cr + si, ci - sr]
                top += [cr - si, ci + sr]
            low_powers = powers(low)
            cross[start : start + rows, :] = low_powers[0]
            diff[start : start + rows, :] = low_powers[1]
            top_powers = powers(top)
            high[0, start : start + rows, :] = top_powers[0]
            high[1, start : start + rows, :] = top_powers[1]

    limits = sorted({min(amount, groups) for amount in (2, 4, 6, groups)})
    for least, most in zip([-1] + limits[:-1], limits):
        pl.when((used > least) & (used <= most))(functools.partial(transform, most))

    backwards = 7 - lax.broadcasted_iota(jnp.int32, (8, pixels), 0)
    for row in range(0, half, 8):
        for which, target in enumerate((cross, diff)):
            piece = high[which, half - row - 7 : half - row + 1, :]
            target[half + row : half + row + 8, :] = jnp.take_along_axis(piece, backwards, axis=0)

    for parity in range(2):

        listed = (step * 2 + parity) * capacity

        def clean(index, _):
            columns = slice(2 * parity * pixels, 2 * (parity + 1) * pixels)
            for begin in halves(listed + index)[1]:
                spot = spot_of[lax.div(begin, lanes)]
                target = pl.ds(pl.multiple_of(spot * lanes + lax.rem(begin, lanes), width), width)
                acc[target, columns] = jnp.zeros((width, 2 * pixels), acc.dtype)
                grid[target, columns] = jnp.zeros((width, 2 * pixels), grid.dtype)
            return 0

        lax.fori_loop(0, count[step * 2 + parity], clean, 0)


def on_device(visibility, kernel, block_tile, block_chan, tile_owner, inv_cov):
    n_uv = lax.axis_size("uv")
    n_ch = lax.axis_size("channel")
    n_par = lax.axis_size("parity")
    samples = visibility[0, 0]
    weights = kernel[0, 0]
    blocks, doubled, _ = samples.shape
    pixels = weights.shape[2]
    channels = inv_cov.shape[0]
    tile_total = tile_owner.shape[0]
    group_tiles = tile_total // n_uv // n_ch
    out_tiles = group_tiles // n_par
    dests = n_uv * n_ch
    slots = max(1, 2 * blocks // dests)
    smem = pl.BlockSpec(memory_space=pltpu.SMEM)
    vmem = pl.BlockSpec(memory_space=pltpu.VMEM)
    anywhere = pl.BlockSpec(memory_space=pl.ANY)
    lines = math.gcd(blocks, 4)

    outgoing, meta = pl.pallas_call(
        lambda *refs: pack_kernel(n_ch, slots, group_tiles, channels, *refs[:-1], lines, refs[-1]),
        out_shape=(
            jax.ShapeDtypeStruct((dests, slots, doubled, pixels), jnp.bfloat16),
            jax.ShapeDtypeStruct((dests, 1, 128), jnp.int32),
        ),
        in_specs=[pl.BlockSpec(memory_space=pltpu.HBM)] * 5,
        out_specs=(vmem, smem),
        scratch_shapes=[
            pltpu.SMEM((blocks,), jnp.int32),
            pltpu.SMEM((blocks,), jnp.int32),
            pltpu.SMEM((tile_total,), jnp.int32),
            pltpu.VMEM(samples.shape, samples.dtype),
            pltpu.VMEM(weights.shape, weights.dtype),
            pltpu.SMEM((tile_total,), jnp.int32),
            pltpu.SMEM((n_uv,), jnp.int32),
            pltpu.SMEM((dests,), jnp.int32),
            pltpu.SemaphoreType.DMA((4 + lines,)),
        ],
        compiler_params=pltpu.CompilerParams(vmem_limit_bytes=60 << 20),
        name="pack_terms",
    )(block_tile[0, 0], block_chan[0, 0], tile_owner, samples, weights)

    got, got_meta, mix = pl.pallas_call(
        functools.partial(exchange_kernel, n_uv, n_ch),
        out_shape=(
            jax.ShapeDtypeStruct((2, dests, slots, doubled, pixels), jnp.bfloat16),
            jax.ShapeDtypeStruct((2, dests, 1, 128), jnp.int32),
            jax.ShapeDtypeStruct((channels // 128, channels, 128), jnp.bfloat16),
        ),
        in_specs=[anywhere, anywhere, anywhere, vmem],
        out_specs=(anywhere, anywhere, anywhere),
        scratch_shapes=[
            pltpu.VMEM((channels, channels), jnp.float32),
            pltpu.VMEM((channels // 128, channels, 128), jnp.bfloat16),
            pltpu.SemaphoreType.DMA((4,)),
            pltpu.SemaphoreType.DMA((2, dests)),
            pltpu.SemaphoreType.DMA((2, dests)),
            pltpu.SemaphoreType.DMA((2, dests)),
            pltpu.SemaphoreType.DMA((2, dests)),
        ],
        compiler_params=pltpu.CompilerParams(
            collective_id=0, has_side_effects=True, vmem_limit_bytes=57 << 20
        ),
        name="exchange_terms",
    )(outgoing, meta, half_table(channels), inv_cov)

    area = pl.BlockSpec((channels, pixels), lambda t: (0, t))
    return pl.pallas_call(
        functools.partial(power_kernel, n_ch, slots, dests, out_tiles, math.sqrt(channels)),
        grid=(out_tiles,),
        out_shape=(jax.ShapeDtypeStruct((channels, out_tiles * pixels), jnp.float32),) * 2,
        in_specs=[smem, vmem, vmem],
        out_specs=(area, area),
        scratch_shapes=[
            pltpu.VMEM((channels, 4 * pixels), jnp.float32),
            pltpu.VMEM((channels, 4 * pixels), jnp.bfloat16),
            pltpu.VMEM((2, channels // 2 + 8, pixels), jnp.float32),
            pltpu.SMEM((2 * out_tiles + 1,), jnp.int32),
            pltpu.SMEM((2 * out_tiles * dests * slots + 1,), jnp.int32),
            pltpu.SMEM((2 * out_tiles * dests * slots + 1,), jnp.int32),
            pltpu.SMEM((channels // 128,), jnp.int32),
            pltpu.SMEM((channels // 128,), jnp.int32),
        ],
        compiler_params=pltpu.CompilerParams(vmem_limit_bytes=60 << 20),
        name="power_spectra",
    )(got_meta, got.reshape(2 * dests * slots, doubled, pixels), mix)


def solution(mesh):
    placed = (
        P("parity", "channel", "uv", None, None),
        P("parity", "channel", "uv", None, None),
        P("parity", "channel", "uv"),
        P("parity", "channel", "uv"),
        P(),
        P(),
    )
    return jax.shard_map(
        on_device,
        mesh=mesh,
        in_specs=placed,
        out_specs=(P(None, ("uv", "channel", "parity")), P(None, ("uv", "channel", "parity"))),
        check_vma=False,
    )
```
